32 devices in a mesh: rep: 4 (over z), shard: 8 (over y, x, core).
Axes of the slice: x: 2, y: 2, z: 4, core: 2. Of those that a mesh axis runs over, the one named last changes fastest.
Arguments:
- tokens: bfloat16 [4096, 2048], P(('rep', 'shard')), may hold values from -6 to 6
- norm_gains: bfloat16 [4, 2048], P(None, 'shard'), may hold values from 0.5 to 1.5
- w_qkv: bfloat16 [2048, 6144], P('shard'), may hold values from -0.125 to 0.125
- w_attn_out: bfloat16 [2048, 2048], P('shard'), may hold values from -0.5 to 0.5
- w_in: bfloat16 [16, 2048, 2048], P(None, 'shard'), may hold values from -0.125 to 0.125
- w_out: bfloat16 [16, 2048, 1024], P(None, 'shard'), may hold values from -0.75 to 0.75
- route_gates: float32 [4096, 8], P(('rep', 'shard')), may hold values from 0.06 to 0.2
- routes: int32 [4096, 8], P(('rep', 'shard')), may hold values from 0 to 15, all different within a row; in each aligned block of 128 rows (0 to 127, 128 to 255, ...) at most 72 rows name the same one
- prefix: int32 [32], P(('rep', 'shard')), may hold values from 12 to 64
- cotangent: bfloat16 [4096, 2048], P(('rep', 'shard')), may hold values from -6 to 6
Outputs:
- layer_out: bfloat16 [4096, 2048], P(('rep', 'shard'))
- tokens_grad: bfloat16 [4096, 2048], P(('rep', 'shard'))
- gains_grad: float32 [4, 2048], P(None, 'shard')
- qkv_grad: float32 [2048, 6144], P('shard')
- attn_out_grad: float32 [2048, 2048], P('shard')
- in_grad: float32 [16, 2048, 2048], P(None, 'shard')
- out_grad: float32 [16, 2048, 1024], P(None, 'shard')
The draws below stay inside these ranges and needn't reach their ends.
Inputs may be any that keep to these rules, and one draw needn't show every extreme that they name: `routes`: each row names 8 different experts; among the rows of one device no expert is named more than 72 times, a bound that some block reaches.
All inputs are finite; a program needn't handle non-finite values.
Results may differ from the reference program's by a relative error of at most 0.02.
Values may be sent and summed in bfloat16 or wider, within the bound.
No kernel may reach another device: no remote copies, remote signals or barrier semaphores. Data moves between devices by JAX's collectives and lax.ppermute only.
A program may use at most 320 MiB of HBM per device.

```python
import math
import jax
import jax.numpy as jnp
import numpy as np
from jax import lax

D = 2048
HEADS = 16
HEAD_DIM = 128
FF = 1024
EXPERTS = 16
TOPK = 8
TOK_DEV = 128
CAP = 72
SEQS = 32
TOKENS = 4096


def set_ends(result, own_key, low, high):
    spot = [jax.random.randint(jax.random.fold_in(own_key, axis), (), 0, length) for axis, length in enumerate(result.shape)]
    widest = result.shape.index(max(result.shape))
    next_to = spot[:widest] + [(spot[widest] + 1) % result.shape[widest]] + spot[widest + 1:]
    return result.at[tuple(spot)].set(low).at[tuple(next_to)].set(high)


def block_levels(rng, extent, split, low, top_value):
    level, own = 1.0, jax.random.fold_in(rng, 6)
    for dim, shards_of in split:
        draws = jnp.exp(jax.random.uniform(jax.random.fold_in(own, dim), (shards_of,), jnp.float32, low / len(split), top_value / len(split)))
        level = level * jnp.repeat(draws, extent[dim] // shards_of).reshape([-1 if axis == dim else 1 for axis in range(len(extent))])
    return level


def deal_out(key, own, number, rows, count, top, reach, lean):
    order = jax.random.permutation(key, count)
    heavy_load, common = portions_of(count, rows * top, reach, lean, True), portions_of(count, rows * top, reach, lean, False)
    places = jnp.arange(count)

    def named(lengths, rotation):
        used = int((lengths > 0).sum())
        fixed = max(1, used // 4)
        shifted = fixed + (places - fixed + rotation * (used - fixed)) % max(1, count - fixed)
        return jnp.zeros((count,), jnp.int32).at[order[jnp.where(places < fixed, places, shifted)]].set(jnp.asarray(lengths, jnp.int32))

    lengths = jnp.where(number % 4 == 0, named(heavy_load, number // 4), named(common, number - number // 4 - 1))
    mixed = jax.random.permutation(jax.random.fold_in(own, 3), count)
    source_of, taker = mixed[0:count // 2 * 2:2], mixed[1:count // 2 * 2:2]
    room = jnp.minimum(lengths[source_of] - 1, reach - lengths[taker]) // 2
    room = jnp.where((source_of == order[0]) | (taker == order[0]) | (lengths[taker] == 0), 0, jnp.maximum(room, 0))
    shifted = jax.random.randint(jax.random.fold_in(own, 4), (count // 2,), 0, 1 << 20) % (room + 1)
    lengths = lengths.at[source_of].add(-shifted).at[taker].add(shifted)
    items = jnp.searchsorted(jnp.cumsum(lengths), jnp.arange(rows * top), side="right").astype(jnp.int32)
    listing = items.reshape(top, rows).T
    listing = listing[jax.random.permutation(jax.random.fold_in(own, 1), rows)]
    rotation = jax.random.randint(jax.random.fold_in(own, 2), (rows, 1), 0, top)
    return jnp.take_along_axis(listing, (jnp.arange(top)[None, :] + rotation) % top, axis=1)


def portions_of(number_of, total, limit, skew, full):
    portions = [(1 << 20) // math.isqrt(grade ** skew) + 1 for grade in range(1, number_of + 1)]
    largest = limit if full else min(limit, max(-(-total // number_of), total * portions[0] // sum(portions)))
    least = 1 if total - largest >= number_of - 1 else 0
    given, rest = [largest] + [least] * (number_of - 1), total - largest - least * (number_of - 1)
    while rest > 0:
        movable = [i for i in range(1, number_of) if given[i] < largest] or [i for i in range(1, number_of) if given[i] < limit]
        whole, remaining = sum([portions[i] for i in movable]), rest
        for i in movable:
            more = min(limit - given[i], max(1, remaining * portions[i] // whole), rest)
            given[i] = given[i] + more
            rest = rest - more
    return np.array(given)


def bell_draw(own_key, dims, deviation, limit, cuts=(), held_as=jnp.bfloat16):
    entries = deviation * jax.random.normal(own_key, dims, jnp.float32)
    if cuts:
        entries = entries * block_levels(own_key, dims, cuts, -0.22, 0.18)
    return jnp.clip(entries, -limit, limit).astype(held_as)


def setup_inputs(seed: int = 0) -> dict:
    arg_keys = jax.random.split(jax.random.key(seed), 11)
    tokens = bell_draw(arg_keys[0], (TOKENS, D), 1.0, 6.0, ((0, 32),))
    norm_gains = jnp.clip(1.0 + 0.1 * jax.random.normal(arg_keys[1], (4, D), jnp.float32), 0.5, 1.5).astype(jnp.bfloat16)
    w_qkv = bell_draw(arg_keys[2], (D, 3 * D), D ** -0.5, 0.125, ((0, 8),))
    w_attn_out = bell_draw(arg_keys[3], (D, D), (D // 16) ** -0.5, 0.5, ((0, 8),))
    w_in = bell_draw(arg_keys[4], (EXPERTS, D, 2 * FF), D ** -0.5, 0.125, ((1, 8),))
    w_out = bell_draw(arg_keys[5], (EXPERTS, D, FF), (FF // 16) ** -0.5, 0.75, ((1, 8),))
    route_gates = jnp.clip(jnp.exp(math.log(0.2) - 1.2039728 * jax.random.uniform(arg_keys[6], (TOKENS, TOPK), jnp.float32) ** block_levels(arg_keys[6], (TOKENS, TOPK), ((0, 32),), -0.2, 0.2)), 0.06, 0.2)
    routes_keys = jax.random.split(jax.random.fold_in(arg_keys[7], 1), TOKENS // TOK_DEV)
    routes_turns = jax.random.permutation(jax.random.fold_in(arg_keys[7], 3), TOKENS // TOK_DEV)
    routes = jax.vmap(lambda own, number: deal_out(jax.random.fold_in(arg_keys[7], 2), own, number, TOK_DEV, EXPERTS, TOPK, CAP, 1))(routes_keys, routes_turns).reshape((TOKENS, TOPK))
    prefix = set_ends(jax.random.randint(arg_keys[8], (SEQS,), TOK_DEV // 10, TOK_DEV // 2 + 1), jax.random.fold_in(arg_keys[8], 1), TOK_DEV // 10, (TOK_DEV // 2 + 1) - 1).astype(jnp.int32)
    cotangent = bell_draw(arg_keys[9], (TOKENS, D), 1.0, 6.0, ((0, 32),))
    return dict(tokens=tokens, norm_gains=norm_gains, w_qkv=w_qkv, w_attn_out=w_attn_out, w_in=w_in, w_out=w_out, route_gates=route_gates, routes=routes, prefix=prefix, cotangent=cotangent)


@jax.custom_vjp
def low(v):
    return lax.optimization_barrier(v.astype(jnp.bfloat16)).astype(jnp.float32)

@jax.custom_vjp
def low_back(v):
    return v

def low_keep(v):
    return (low(v), None)

def low_pass(kept, grad):
    return (grad,)

def back_keep(v):
    return (v, None)

def back_low(kept, grad):
    return (low(grad),)
low.defvjp(low_keep, low_pass)
low_back.defvjp(back_keep, back_low)
highest = lax.Precision.HIGHEST
epsilon = 1e-05
masked_value = -1e+30

def rms_norm(vector, norm_gain):
    return vector * lax.rsqrt(lax.optimization_barrier(jnp.mean(vector * vector, axis=-1, keepdims=True)) + epsilon) * norm_gain

def rotate(vector, direction):
    length = vector.shape[0]
    halfway = vector.shape[-1] // 2
    frequency = 10000.0 ** (-jnp.arange(halfway, dtype=jnp.float32) / halfway)
    angles = jnp.arange(length, dtype=jnp.float32)[:, None] * frequency[None, :]
    cosine = jnp.cos(angles)[:, None, :]
    sine_part = direction * jnp.sin(angles)[:, None, :]
    first_half = vector[..., :halfway]
    second_half = vector[..., halfway:]
    return jnp.concatenate([first_half * cosine - second_half * sine_part, second_half * cosine + first_half * sine_part], axis=-1)

def dispatch(routes):
    length = routes.shape[0]
    flat_routes = routes.reshape(-1).astype(jnp.int32)
    onehot = (flat_routes[:, None] == jnp.arange(EXPERTS, dtype=jnp.int32)[None, :]).astype(jnp.int32)
    before = jnp.cumsum(onehot, axis=0) - onehot
    in_expert = lax.optimization_barrier(jnp.sum(before * onehot, axis=1))
    assign_slot = (flat_routes * CAP + in_expert).astype(jnp.int32)
    token_index = (jnp.arange(length * TOPK, dtype=jnp.int32) // TOPK).astype(jnp.int32)
    slot_token = jnp.zeros((EXPERTS * CAP,), jnp.int32).at[assign_slot].set(token_index)
    slot_live = jnp.zeros((EXPERTS * CAP,), jnp.float32).at[assign_slot].set(1.0)
    return (slot_token, slot_live, assign_slot)

def forward(token_rows, gain_rows, qkv_weight, attn_weight, expert_in_w, expert_out_w, seq_gates, seq_routes, seq_prefix):
    length = token_rows.shape[0]
    normed = low(rms_norm(token_rows, gain_rows[0]))
    project = low_back(jnp.dot(normed, qkv_weight, precision=highest))
    queries = low(rotate(rms_norm(project[:, :D], gain_rows[1]).reshape(length, HEADS, HEAD_DIM), 1.0))
    key_rows = low(rotate(rms_norm(project[:, D:2 * D], gain_rows[2]).reshape(length, HEADS, HEAD_DIM), 1.0))
    values = low(project[:, 2 * D:].reshape(length, HEADS, HEAD_DIM))
    positions = jnp.arange(length, dtype=jnp.int32)
    allowed = (positions[None, :] <= positions[:, None]) | (positions[None, :] < seq_prefix)
    scores = low_back(jnp.einsum('qhd,khd->hqk', queries, key_rows, precision=highest) / jnp.sqrt(jnp.float32(HEAD_DIM)))
    masked = jnp.where(allowed[None], scores, masked_value)
    attn_probs = low(jax.nn.softmax(masked, axis=-1))
    attended = jnp.einsum('hqk,khd->qhd', attn_probs, values, precision=highest).reshape(length, D)
    attended = low_back(low(attended))
    branch = low_back(jnp.dot(attended, attn_weight, precision=highest))
    middle = token_rows + branch
    normed_ffn = low(rms_norm(middle, gain_rows[3]))
    slot_token, slot_live, assign_slot = dispatch(seq_routes)
    expert_in = low_back(normed_ffn[slot_token] * slot_live[:, None]).reshape(EXPERTS, CAP, D)
    gate_up = low_back(jnp.einsum('ecd,edf->ecf', expert_in, expert_in_w, precision=highest))
    hidden = low(jax.nn.silu(gate_up[..., :FF]) * gate_up[..., FF:])
    expert_out = low_back(low(jnp.einsum('ecf,edf->ecd', hidden, expert_out_w, precision=highest)))
    picked = expert_out.reshape(EXPERTS * CAP, D)[assign_slot].reshape(length, TOPK, D)
    expert_mix = lax.optimization_barrier(jnp.sum(picked * seq_gates[:, :, None], axis=1))
    return middle + expert_mix

def reference(tokens, norm_gains, w_qkv, w_attn_out, w_in, w_out, route_gates, routes, prefix, cotangent):
    seq_count = tokens.shape[0] // TOK_DEV
    weights = (norm_gains.astype(jnp.float32), w_qkv.astype(jnp.float32), w_attn_out.astype(jnp.float32), w_in.astype(jnp.float32), w_out.astype(jnp.float32))

    def one_sequence(totals, pieces):
        seq_tokens, seq_gates, seq_routes, seq_prefix, seq_cotangent = pieces

        def layer_only(token_rows, gain_rows, qkv_weight, attn_weight, expert_in_w, expert_out_w):
            return forward(token_rows, gain_rows, qkv_weight, attn_weight, expert_in_w, expert_out_w, seq_gates, seq_routes, seq_prefix)
        output, pullback = jax.vjp(layer_only, seq_tokens.astype(jnp.float32), *weights)
        gradients = pullback(seq_cotangent.astype(jnp.float32))
        totals = tuple((running + update for running, update in zip(totals, gradients[1:])))
        return (totals, (output.astype(jnp.bfloat16), gradients[0].astype(jnp.bfloat16)))
    starting = tuple((jnp.zeros(weight.shape, jnp.float32) for weight in weights))
    shaped = (tokens.reshape(seq_count, TOK_DEV, D), route_gates.reshape(seq_count, TOK_DEV, TOPK), routes.reshape(seq_count, TOK_DEV, TOPK), prefix, cotangent.reshape(seq_count, TOK_DEV, D))
    totals, (outputs, grad_tokens) = lax.scan(one_sequence, starting, shaped)
    return (outputs.reshape(-1, D), grad_tokens.reshape(-1, D), totals[0], totals[1], totals[2], totals[3], totals[4])
```

```python
import math

import jax
import jax.numpy as jnp
from jax import lax
from jax.sharding import PartitionSpec as P

D = 2048
HEADS = 16
HEAD_DIM = 128
FF = 1024
EXPERTS = 16
TOPK = 8
CAP = 72

epsilon = 1e-05
masked_value = -1e30
bf16 = jnp.bfloat16
f32 = jnp.float32


def swap(array, axis, distance):
    count = lax.axis_size(axis)
    return lax.ppermute(array, axis, [(i, i ^ distance) for i in range(count)])


def gather_chips(block):
    chips = lax.axis_size("shard") // 2
    return jnp.stack([block] + [swap(block, "shard", 2 * m) for m in range(1, chips)])


def join_cores(blocks):
    return jnp.stack([blocks, swap(blocks, "shard", 1)])


def gather_group(block):
    return join_cores(gather_chips(block)).reshape((-1,) + block.shape)


def gather_everywhere(block):
    reps = lax.axis_size("rep")
    mine = gather_chips(block)
    far = jnp.stack([swap(mine, "rep", r) for r in range(1, reps)])
    near = join_cores(mine).reshape((-1,) + block.shape)
    far_both = jnp.stack([far, swap(far, "shard", 1)], axis=1)
    return near, far_both.reshape((-1,) + block.shape)


def scatter_group(partial):
    count = partial.shape[0]
    half = count // 2
    partial = partial.astype(bf16)
    chip_sum = partial[:half].astype(f32) + swap(partial[half:], "shard", 1).astype(f32)
    total = chip_sum[0]
    sent = chip_sum.astype(bf16)
    for m in range(1, half):
        total = total + swap(sent[m], "shard", 2 * m).astype(f32)
    return total


def sum_group(small):
    kinds, count, length = small.shape
    bits = count.bit_length() - 1
    small = small.reshape((kinds,) + (2,) * bits + (length,))
    for bit in range(bits):
        axis = 1 if bit == 0 else 1 + bits - bit
        small = small + jnp.flip(swap(small, "shard", 1 << bit), axis)
    return small.reshape(kinds, count, length)


def exchange(array):
    return lax.all_to_all(array, "shard", split_axis=0, concat_axis=0, tiled=True)


def norm_parts(vector):
    inverse = lax.rsqrt(jnp.mean(vector * vector, axis=-1, keepdims=True) + epsilon)
    return (vector * inverse, inverse)


def norm_back(upstream, unit_rows, inverse):
    return inverse * (upstream - unit_rows * jnp.mean(upstream * unit_rows, axis=-1, keepdims=True))


def rope_tables(length):
    halfway = HEAD_DIM // 2
    frequency = 10000.0 ** (-jnp.arange(halfway, dtype=f32) / halfway)
    angles = jnp.arange(length, dtype=f32)[:, None] * frequency[None, :]
    return jnp.cos(angles), jnp.sin(angles)


def rotate(vector, cosine, sine):
    halfway = HEAD_DIM // 2
    first_half = vector[..., :halfway]
    second_half = vector[..., halfway:]
    return jnp.concatenate(
        [first_half * cosine - second_half * sine, second_half * cosine + first_half * sine],
        axis=-1,
    )


def dot(a, b, contract):
    return lax.dot_general(a, b, ((contract[0], contract[1]), ((), ())), preferred_element_type=f32)


def body(
    tokens, norm_gains, w_qkv, w_attn_out, w_in, w_out, route_gates, routes, prefix, cotangent
):
    length = tokens.shape[0]
    group = lax.axis_size("shard")
    reps = lax.axis_size("rep")
    local_experts = EXPERTS // group
    local_heads = HEADS // group
    width = D // group
    rank = lax.axis_index("shard")
    score_scale = 1.0 / math.sqrt(HEAD_DIM)

    qkv_cols = exchange(
        w_qkv.reshape(width, 3, group, width).transpose(2, 0, 1, 3)
    ).reshape(D, 3 * width)
    gains_full = (
        exchange(jnp.broadcast_to(norm_gains[None], (group,) + norm_gains.shape))
        .transpose(1, 0, 2)
        .reshape(4, D)
        .astype(f32)
    )
    weights_in, weights_out = [], []
    for j in range(local_experts):
        rows = slice(j * group, (j + 1) * group)
        weights_in.append(exchange(w_in[rows]).reshape(D, 2 * FF))
        weights_out.append(exchange(w_out[rows]).reshape(D, FF))

    named = routes[:, :, None] == jnp.arange(EXPERTS, dtype=jnp.int32)[None, None, :]
    member = jnp.any(named, axis=1)
    gate_of = jnp.sum(jnp.where(named, route_gates[:, :, None], 0.0), axis=1)
    earlier = (jnp.arange(length)[:, None] > jnp.arange(length)[None, :]).astype(f32)
    place = jnp.dot(earlier, member.astype(f32))
    place = jnp.where(member, place, -1.0)
    tables = jnp.stack([place.T, gate_of.T])

    tokens_near = gather_group(tokens).reshape(group * length, D)
    prefix_near = gather_group(jnp.broadcast_to(prefix[:, None], (8, 128)))[:, 0, 0]
    tables_near, tables_far = gather_everywhere(tables)
    dy_near, dy_far = gather_everywhere(cotangent)

    unit_first, inverse_first = norm_parts(tokens_near.astype(f32))
    normed = (unit_first * gains_full[0]).astype(bf16)
    project = jnp.dot(normed, qkv_cols, preferred_element_type=f32)
    q_raw, k_raw = project[:, :width], project[:, width : 2 * width]
    squares = jnp.stack([jnp.sum(q_raw * q_raw, axis=-1), jnp.sum(k_raw * k_raw, axis=-1)])
    inverse_qk = lax.rsqrt(
        sum_group(squares.reshape(2, group, length)).reshape(2, -1) / D + epsilon
    )
    inverse_query, inverse_keys = inverse_qk[0][:, None], inverse_qk[1][:, None]
    unit_query, unit_keys = q_raw * inverse_query, k_raw * inverse_keys
    own_gains = norm_gains.astype(f32)
    cosine, sine = rope_tables(length)

    def heads_of(array):
        return array.reshape(group, length, local_heads, HEAD_DIM).transpose(0, 2, 1, 3)

    def rows_of(array):
        return array.transpose(0, 2, 1, 3).reshape(group * length, width)

    queries = rotate(heads_of(unit_query * own_gains[1]), cosine, sine).astype(bf16)
    key_rows = rotate(heads_of(unit_keys * own_gains[2]), cosine, sine).astype(bf16)
    values = heads_of(project[:, 2 * width :].astype(bf16))
    positions = jnp.arange(length, dtype=jnp.int32)
    allowed = (positions[None, None, :] <= positions[None, :, None]) | (
        positions[None, None, :] < prefix_near[:, None, None]
    )
    scores = jnp.einsum("nhqd,nhkd->nhqk", queries, key_rows, preferred_element_type=f32)
    masked = jnp.where(allowed[:, None], scores * score_scale, masked_value)
    top_score = jnp.max(masked, axis=-1, keepdims=True)
    powers = jnp.exp(masked - top_score)
    attn_exact = powers / jnp.sum(powers, axis=-1, keepdims=True)
    attn_probs = attn_exact.astype(bf16)
    attended = rows_of(
        jnp.einsum("nhqk,nhkd->nhqd", attn_probs, values, preferred_element_type=f32)
    ).astype(bf16)
    branch_part = jnp.dot(attended, w_attn_out, preferred_element_type=f32)
    branch = scatter_group(branch_part.reshape(group, length, D))
    middle = tokens.astype(f32) + branch
    unit_second, inverse_second = norm_parts(middle)
    normed_ffn = (unit_second * gains_full[3]).astype(bf16)
    ffn_near, ffn_far = gather_everywhere(normed_ffn)

    ffn_all = jnp.concatenate([ffn_near, ffn_far])
    dy_all = jnp.concatenate([dy_near, dy_far])
    tables_all = jnp.concatenate([tables_near, tables_far])
    near = group * CAP
    mix_part = 0.0
    grad_ffn_part = 0.0
    sent_in, sent_out = [], []
    for j in range(local_experts):
        expert = j * group + rank
        mine = lax.dynamic_index_in_dim(tables_all, expert, axis=2, keepdims=False)
        place_of, gates_of = mine[:, 0], mine[:, 1]
        hit = place_of[:, None, :] == jnp.arange(CAP, dtype=f32)[None, :, None]
        pick = hit.astype(bf16)
        weighted = jnp.where(hit, gates_of[:, None, :], 0.0).astype(bf16)
        slot_rows = (
            jnp.einsum("nst,ntd->nsd", pick, ffn_all, preferred_element_type=f32)
            .astype(bf16)
            .reshape(-1, D)
        )
        slot_grads = (
            jnp.einsum("nst,ntd->nsd", weighted, dy_all, preferred_element_type=f32)
            .astype(bf16)
            .reshape(-1, D)
        )
        gate_up = jnp.dot(slot_rows, weights_in[j], preferred_element_type=f32)
        gate, up = gate_up[:, :FF], gate_up[:, FF:]
        sigmoid_gate = jax.nn.sigmoid(gate)
        silu_gate = gate * sigmoid_gate
        hidden = (silu_gate * up).astype(bf16)
        grad_hidden = jnp.dot(slot_grads, weights_out[j], preferred_element_type=f32)
        grad_gate = grad_hidden * up * sigmoid_gate * (1.0 + gate * (1.0 - sigmoid_gate))
        grad_up = grad_hidden * silu_gate
        grad_gate_up = jnp.concatenate([grad_gate, grad_up], axis=-1).astype(bf16)
        out_rows = dot(hidden[:near], weights_out[j], ((1,), (1,))).astype(bf16)
        mix_part = mix_part + jnp.einsum(
            "nst,nsd->ntd",
            weighted[:group],
            out_rows.reshape(group, CAP, D),
            preferred_element_type=f32,
        )
        grad_rows = dot(grad_gate_up[:near], weights_in[j], ((1,), (1,))).astype(bf16)
        grad_ffn_part = grad_ffn_part + jnp.einsum(
            "nst,nsd->ntd",
            pick[:group],
            grad_rows.reshape(group, CAP, D),
            preferred_element_type=f32,
        )
        grad_out = dot(slot_grads, hidden, ((0,), (0,))).astype(bf16)
        grad_in = dot(slot_rows, grad_gate_up, ((0,), (0,))).astype(bf16)
        sent_out.append(exchange(grad_out.reshape(group, width, FF)))
        sent_in.append(exchange(grad_in.reshape(group, width, 2 * FF)))
    in_grad = jnp.concatenate(sent_in).astype(f32)
    out_grad = jnp.concatenate(sent_out).astype(f32)
    output = (middle + scatter_group(mix_part)).astype(bf16)

    grad_normed_ffn = scatter_group(grad_ffn_part)
    grad_gain_ffn = jnp.sum(grad_normed_ffn * unit_second, axis=0)
    grad_middle = cotangent.astype(f32) + norm_back(
        grad_normed_ffn * gains_full[3], unit_second, inverse_second
    )
    grad_branch = gather_group(grad_middle.astype(bf16)).reshape(group * length, D)
    grad_attended = heads_of(dot(grad_branch, w_attn_out, ((1,), (1,))).astype(bf16))
    grad_attn_out = dot(attended, grad_branch, ((0,), (0,)))
    grad_values = jnp.einsum(
        "nhqk,nhqd->nhkd", attn_probs, grad_attended, preferred_element_type=f32
    )
    grad_probs = jnp.einsum("nhqd,nhkd->nhqk", grad_attended, values, preferred_element_type=f32)
    row_dot = jnp.sum(attn_exact * grad_probs, axis=-1, keepdims=True)
    grad_scores = (attn_exact * (grad_probs - row_dot)).astype(bf16)
    grad_queries = (
        jnp.einsum("nhqk,nhkd->nhqd", grad_scores, key_rows, preferred_element_type=f32)
        * score_scale
    )
    grad_keys = (
        jnp.einsum("nhqk,nhqd->nhkd", grad_scores, queries, preferred_element_type=f32)
        * score_scale
    )
    grad_query_unit = rows_of(rotate(grad_queries, cosine, -sine))
    grad_keys_unit = rows_of(rotate(grad_keys, cosine, -sine))
    grad_gain_query = jnp.sum(grad_query_unit * unit_query, axis=0)
    grad_gain_keys = jnp.sum(grad_keys_unit * unit_keys, axis=0)
    grad_query_unit = grad_query_unit * own_gains[1]
    grad_keys_unit = grad_keys_unit * own_gains[2]
    means = sum_group(
        jnp.stack(
            [
                jnp.sum(grad_query_unit * unit_query, axis=-1),
                jnp.sum(grad_keys_unit * unit_keys, axis=-1),
            ]
        ).reshape(2, group, length)
    ).reshape(2, -1) / D
    grad_query_raw = inverse_query * (grad_query_unit - unit_query * means[0][:, None])
    grad_keys_raw = inverse_keys * (grad_keys_unit - unit_keys * means[1][:, None])
    grad_project = jnp.concatenate(
        [grad_query_raw, grad_keys_raw, rows_of(grad_values)], axis=1
    ).astype(bf16)
    grad_normed = scatter_group(
        dot(grad_project, qkv_cols, ((1,), (1,))).reshape(group, length, D)
    )
    unit_own, inverse_own = norm_parts(tokens.astype(f32))
    grad_gain_first = jnp.sum(grad_normed * unit_own, axis=0)
    tokens_grad = (
        grad_middle + norm_back(grad_normed * gains_full[0], unit_own, inverse_own)
    ).astype(bf16)

    grad_qkv = dot(normed, grad_project, ((0,), (0,))).astype(bf16)
    slices = grad_qkv.reshape(group, reps, width // reps, 3 * width).transpose(1, 0, 2, 3)
    arrived = lax.all_to_all(
        slices.reshape(reps * group, width // reps, 3 * width),
        ("rep", "shard"),
        split_axis=0,
        concat_axis=0,
        tiled=True,
    ).reshape(reps, group, width // reps, 3, width)
    qkv_slice = (
        jnp.sum(arrived.astype(f32), axis=0)
        .transpose(1, 2, 0, 3)
        .reshape(width // reps, 3 * D)
        .astype(bf16)
    )
    qkv_grad = lax.all_gather(qkv_slice, "rep", axis=0, tiled=True).astype(f32)
    attn_arrived = lax.all_to_all(
        grad_attn_out.astype(bf16), "rep", split_axis=0, concat_axis=0, tiled=True
    ).reshape(reps, width // reps, D)
    attn_slice = jnp.sum(attn_arrived.astype(f32), axis=0).astype(bf16)
    attn_out_grad = lax.all_gather(attn_slice, "rep", axis=0, tiled=True).astype(f32)

    whole = jnp.stack([grad_gain_first, grad_gain_ffn]).reshape(2, group, width).transpose(1, 0, 2)
    owned = jnp.sum(exchange(whole), axis=0)
    gains_grad = lax.psum(
        jnp.stack([owned[0], grad_gain_query, grad_gain_keys, owned[1]]), "rep"
    )
    return (output, tokens_grad, gains_grad, qkv_grad, attn_out_grad, in_grad, out_grad)


def solution(mesh):
    placed = (
        P(("rep", "shard"), None),
        P(None, "shard"),
        P("shard", None),
        P("shard", None),
        P(None, "shard", None),
        P(None, "shard", None),
        P(("rep", "shard"), None),
        P(("rep", "shard"), None),
        P(("rep", "shard")),
        P(("rep", "shard"), None),
    )
    return jax.shard_map(
        body,
        mesh=mesh,
        in_specs=placed,
        out_specs=(
            P(("rep", "shard"), None),
            P(("rep", "shard"), None),
            P(None, "shard"),
            P("shard", None),
            P("shard", None),
            P(None, "shard", None),
            P(None, "shard", None),
        ),
        check_vma=False,
    )
```
